32 devices in a mesh: sweep: 4 (over x, core), nd: 8 (over z, y).
Axes of the slice: x: 2, y: 2, z: 4, core: 2. Of those that a mesh axis runs over, the one named last changes fastest.
Arguments:
- f_int: float32 [4, 4, 262144], P('sweep', None, 'nd'), may hold values from -6 to 6
- f_sep: float32 [4, 4, 8192], P('sweep', None, 'nd'), may hold values from -6 to 6
- leaf_inverse: bfloat16 [4, 2048, 128, 128], P('sweep', 'nd'), may hold values from -6 to 6
- sep_inverse: bfloat16 [4, 64, 128, 128], P('sweep', 'nd'), may hold values from -6 to 6
- sep_map: int32 [4, 16384], P('sweep', 'nd'), may hold values from 0 to 8191
- couple: float32 [4, 16384], P('sweep', 'nd'), may hold values from 0.5 to 1.4
- trace_coef: float32 [4, 16384], P('sweep', 'nd'), may hold values from 0.5 to 1
Outputs:
- x_int: float32 [4, 4, 262144], P('sweep', None, 'nd')
- x_sep: float32 [4, 4, 8192], P('sweep', None, 'nd')
The draws below stay inside these ranges and needn't reach their ends.
All inputs are finite; a program needn't handle non-finite values.
Results may differ from the reference program's by a relative error of at most 0.0051.
Values sent between devices are 32-bit elements; how exact they have to be, the bound alone decides.
A program may use at most 128 MiB of HBM per device.

```python
import math
import jax
import jax.numpy as jnp
from jax import lax

RHS = 4
PLANES = 16
EDGE = 128
IFC = 2048
BND = 2048
SEPR = 1024
SEP = 8192
LROWS = 262144
SECTIONS = 4
N_ND = 8


def block_draw(key, count):
    first, second = jax.random.split(key, 2)
    eye = jnp.eye(128, dtype=jnp.float32)
    diag = jax.random.uniform(second, (count, 128, 1), jnp.float32, 0.6, 1.4)
    off = jnp.clip(jax.random.normal(first, (count, 128, 128), jnp.float32), -4.0, 4.0) * (0.6 / math.sqrt(128.0))
    return off * (1.0 - eye) + eye * diag


def draw_leaf_inverse(key, part):
    key = jax.random.fold_in(key, 11)
    count = LROWS // 128
    return block_draw(key, SECTIONS * count).reshape(SECTIONS, count, 128, 128).astype(jnp.bfloat16)


def draw_sep_inverse(key, part):
    key = jax.random.fold_in(key, 12)
    count = SEP // 128
    return block_draw(key, SECTIONS * count).reshape(SECTIONS, count, 128, 128).astype(jnp.bfloat16)


def draw_sep_map(key, part):
    key = jax.random.fold_in(key, 13)
    key_rows, key_owner, key_offset, key_linked = jax.random.split(key, 4)
    total = N_ND * BND
    where = jnp.arange(total, dtype=jnp.int32)
    rows = jax.random.randint(key_rows, (SECTIONS, total), 0, SEP, dtype=jnp.int32)
    distance = jax.random.randint(key_owner, (SECTIONS, N_ND, 1, EDGE), 1, N_ND, dtype=jnp.int32)
    leaves = jnp.arange(N_ND, dtype=jnp.int32).reshape(1, N_ND, 1, 1)
    owning = (leaves + distance) % N_ND
    offset = jax.random.randint(key_offset, (SECTIONS, N_ND, 1, EDGE), 0, SEPR, dtype=jnp.int32)
    paired = owning * SEPR + offset
    retained = jax.random.randint(key_linked, (SECTIONS, N_ND, 1, EDGE), 0, 8, dtype=jnp.int32) < 7
    planes = jnp.arange(PLANES, dtype=jnp.int32).reshape(1, 1, PLANES, 1)
    end_planes = (planes == 0) | (planes == PLANES - 1)
    linked = jnp.broadcast_to(retained & end_planes, (SECTIONS, N_ND, PLANES, EDGE)).reshape(SECTIONS, total)
    paired_full = jnp.broadcast_to(paired, (SECTIONS, N_ND, PLANES, EDGE)).reshape(SECTIONS, total)
    rows = jnp.where(linked, paired_full, rows)
    rows = jnp.where(where[None] == 0, 0, rows)
    rows = jnp.where(where[None] == total - 1, SEP - 1, rows)
    return rows.astype(jnp.int32)


def level_of(rng, dims, cuts, low, largest):
    factor_of, own = 1.0, jax.random.fold_in(rng, 6)
    for position, parts in cuts:
        draws = jnp.exp(jax.random.uniform(jax.random.fold_in(own, position), (parts,), jnp.float32, low / len(cuts), largest / len(cuts)))
        factor_of = factor_of * jnp.repeat(draws, dims[position] // parts).reshape([-1 if axis == position else 1 for axis in range(len(dims))])
    return factor_of


def centred(key, dims, deviation, bound, cuts=(), kind=jnp.bfloat16):
    drawn = jax.random.normal(key, dims, jnp.float32) * deviation
    if len(cuts) > 0:
        drawn = level_of(key, dims, cuts, -0.22, 0.18) * drawn
    return jnp.clip(drawn, min=-bound, max=bound).astype(kind)


def setup_inputs(seed: int = 0) -> dict:
    streams_of = jax.random.split(jax.random.key(seed), 8)
    return {
        "f_int": centred(streams_of[0], (SECTIONS, RHS, LROWS), 1.0, 6.0, ((0, 4), (2, 8)), jnp.float32),
        "f_sep": centred(streams_of[1], (SECTIONS, RHS, SEP), 1.0, 6.0, ((0, 4), (2, 8)), jnp.float32),
        "leaf_inverse": draw_leaf_inverse(jax.random.fold_in(streams_of[7], 71), 0),
        "sep_inverse": draw_sep_inverse(jax.random.fold_in(streams_of[7], 71), 0),
        "sep_map": draw_sep_map(jax.random.fold_in(streams_of[7], 71), 0),
        "couple": jnp.clip(jnp.exp(math.log(1.4) - 1.0296194 * jax.random.uniform(streams_of[5], (SECTIONS, N_ND * BND), jnp.float32) ** level_of(streams_of[5], (SECTIONS, N_ND * BND), ((0, 4), (1, 8)), -0.2, 0.2)), 0.5, 1.4),
        "trace_coef": jnp.clip(jnp.exp(math.log(1.0) - 0.6931472 * jax.random.uniform(streams_of[6], (SECTIONS, N_ND * IFC), jnp.float32) ** level_of(streams_of[6], (SECTIONS, N_ND * IFC), ((0, 4), (1, 8)), -0.2, 0.2)), 0.5, 1.0),
    }


def apply_blocks(inverse, vector):
    count = vector.shape[0]
    rounded = lax.optimization_barrier(vector.astype(jnp.bfloat16)).astype(jnp.float32)
    groups = inverse.reshape(N_ND, -1, 128, 128)
    pieces = rounded.reshape(count, N_ND, -1, 128).transpose(1, 0, 2, 3)

    def one_group(pair):
        return jnp.einsum("bij,rbj->rbi", pair[0].astype(jnp.float32), pair[1], precision=lax.Precision.HIGHEST)

    result = lax.map(one_group, (groups, pieces))
    return result.transpose(1, 0, 2, 3).reshape(count, -1)


def reference(f_int, f_sep, leaf_inverse, sep_inverse, sep_map, couple, trace_coef):
    trace = jnp.zeros((RHS, N_ND, IFC), jnp.float32)
    outs_int = []
    outs_sep = []
    for section in range(SECTIONS):
        coef = trace_coef[section].reshape(N_ND, IFC)
        grid = f_int[section].reshape(RHS, N_ND, PLANES, IFC)
        grid = grid.at[:, :, 0, :].add(-coef[None] * trace)
        g_flat = grid.reshape(RHS, LROWS)
        y_all = apply_blocks(leaf_inverse[section], g_flat)
        y_edge = y_all.reshape(RHS, N_ND, PLANES, IFC)[:, :, :, :EDGE].reshape(RHS, N_ND * BND)
        contrib = y_edge * couple[section][None]
        gathered = jnp.zeros((RHS, SEP), jnp.float32).at[:, sep_map[section]].add(contrib)
        sres = f_sep[section] - gathered
        x_sep = apply_blocks(sep_inverse[section], sres)
        picked = x_sep[:, sep_map[section]] * couple[section][None]
        held = g_flat.reshape(RHS, N_ND, PLANES, IFC)
        held = held.at[:, :, :, :EDGE].add(-picked.reshape(RHS, N_ND, PLANES, EDGE))
        x_int = apply_blocks(leaf_inverse[section], held.reshape(RHS, LROWS))
        trace = x_int.reshape(RHS, N_ND, PLANES, IFC)[:, :, PLANES - 1, :]
        outs_int.append(x_int)
        outs_sep.append(x_sep)
    return jnp.stack(outs_int), jnp.stack(outs_sep)
```

```python
import functools

import jax
import jax.numpy as jnp
from jax import lax
from jax.experimental import pallas as pl
from jax.experimental.pallas import tpu as pltpu
from jax.sharding import PartitionSpec as P

MESH = pl.DeviceIdType.MESH
PLANES = 16
B = 128
F32 = jnp.float32
BF16 = jnp.bfloat16


def dot_nt(a, b):
    return lax.dot_general(a, b, (((1,), (1,)), ((), ())), preferred_element_type=F32)


def dot_nn(a, b):
    return lax.dot_general(a, b, (((1,), (0,)), ((), ())), preferred_element_type=F32)


def split(x):
    high = x.astype(BF16)
    return high, (x - high.astype(F32)).astype(BF16)


def one_hot_rows(low, rows=B):
    shape = (rows, low.shape[1])
    return jnp.where(lax.broadcasted_iota(jnp.int32, shape, 0) == low, 1.0, 0.0).astype(BF16)


def kernel(S, n, leaf_hbm, f_hbm, fsep, sepinv, smap, couple, coef, xint, xsep,
           leaf, f, onehot, scat, maps, own0, own15, base_out, base_in, v_in, pick_out, pick_in,
           xall, l240_out, l240_in, aux_out, aux_in, t_out, t_in, g0,
           load_sem, map_s, map_r, base_s, base_r, v_s, v_r, pick_s, pick_r, x_s, x_r, fwd_s, fwd_r):
    columns = f.shape[1]
    plane = f.shape[2] // PLANES
    per = plane // B
    nh = fsep.shape[2] // B
    total = n * nh
    s = lax.axis_index("sweep")
    me = lax.axis_index("nd")
    after = lax.rem(s + 1, S)
    before = lax.rem(s + S - 1, S)
    first = s == 0
    later = s > 0
    feeds = s < S - 1

    loads = [
        pltpu.make_async_copy(f_hbm, f, load_sem.at[0]),
        pltpu.make_async_copy(leaf_hbm.at[:, 0:1], leaf.at[:, 0:1], load_sem.at[1]),
        pltpu.make_async_copy(leaf_hbm.at[PLANES - 1:PLANES, 1:per], leaf.at[PLANES - 1:PLANES, 1:per], load_sem.at[2]),
        pltpu.make_async_copy(leaf_hbm.at[0:PLANES - 1, 1:per], leaf.at[0:PLANES - 1, 1:per], load_sem.at[3]),
    ]
    for load in loads:
        load.start()

    barrier = pltpu.get_barrier_semaphore()
    for k in range(1, n):
        pl.semaphore_signal(barrier, inc=1, device_id={"sweep": s, "nd": lax.rem(me + k, n)}, device_id_type=MESH)
    for k in range(n):
        other = lax.rem(me + k, n)
        pl.semaphore_signal(barrier, inc=1, device_id={"sweep": after, "nd": other}, device_id_type=MESH)
        pl.semaphore_signal(barrier, inc=1, device_id={"sweep": before, "nd": other}, device_id_type=MESH)

    def to(src, dst, send, recv, sweep, nd):
        return pltpu.make_async_remote_copy(
            src_ref=src, dst_ref=dst, send_sem=send, recv_sem=recv,
            device_id={"sweep": sweep, "nd": nd}, device_id_type=MESH)

    def map_copy(k):
        return to(maps.at[0], maps.at[k], map_s.at[k], map_r.at[k], s, lax.rem(me + k, n))

    def base_copy(k):
        other = lax.rem(me + k, n)
        return to(base_out.at[other], base_in.at[k], base_s.at[k], base_r.at[k], s, other)

    def v_copy(k):
        return to(v_in.at[0], v_in.at[k], v_s.at[k], v_r.at[k], s, lax.rem(me + k, n))

    def pick_copy(k):
        return to(pick_out.at[k], pick_in.at[k], pick_s.at[k], pick_r.at[k], after, lax.rem(me + n - k, n))

    def x_copy(k):
        return to(xall.at[me], xall.at[me], x_s.at[k], x_r.at[k], s, lax.rem(me + k, n))

    l240_copy = to(l240_out, l240_in, fwd_s.at[0], fwd_r.at[0], after, me)
    aux_copy = to(aux_out, aux_in, fwd_s.at[1], fwd_r.at[1], after, me)
    t_copy = to(t_out, t_in, fwd_s.at[2], fwd_r.at[2], after, me)

    maps[0, 0:1, :] = smap[0:1, 0:B]
    maps[0, 1:2, :] = smap[0:1, (PLANES - 1) * B:PLANES * B]
    row_map = smap[0:1, :]
    low = jnp.bitwise_and(row_map, B - 1)
    high = jnp.right_shift(row_map, 7)
    hot = one_hot_rows(low)
    onehot[0:B, :] = hot
    onehot[B:2 * B, :] = hot
    for h in range(nh):
        scat[:, h * B:(h + 1) * B] = sepinv[0, h]

    pl.semaphore_wait(barrier, 3 * n - 1)
    for k in range(1, n):
        map_copy(k).start()

    loads[0].wait()
    loads[1].wait()
    aux_out[0:columns, :] = f[0, :, (PLANES - 1) * plane:(PLANES - 1) * plane + B]
    aux_out[columns:columns + 1, :] = couple[0:1, (PLANES - 1) * B:PLANES * B]
    l240_out[...] = leaf[PLANES - 1, 0].astype(F32)

    @pl.when(feeds)
    def _():
        l240_copy.start()
        aux_copy.start()

    parts = [jnp.zeros((columns, B), F32)]
    for p in range(1, PLANES):
        g = f[0, :, p * plane:p * plane + B].astype(BF16)
        parts.append(dot_nt(g, leaf[p, 0]) * couple[0:1, p * B:(p + 1) * B])
    vals = jnp.concatenate(parts, axis=1)
    v_high, v_low = split(vals)
    v_high, v_low = v_high.astype(F32), v_low.astype(F32)
    is_high = lax.broadcasted_iota(jnp.int32, (total, PLANES * B), 0) == high
    rows = []
    for piece in (v_high, v_low):
        for r in range(columns):
            rows.append(jnp.where(is_high, piece[r:r + 1, :], 0.0).astype(BF16))
    spread = dot_nt(jnp.concatenate(rows, axis=0), onehot[0:B, :])
    for r in range(columns):
        both = spread[r * total:(r + 1) * total] + spread[(columns + r) * total:(columns + r + 1) * total]
        base_out[:, r * nh:(r + 1) * nh, :] = both.reshape(n, nh, B)
    for k in range(1, n):
        base_copy(k).start()

    def send_v():
        y0 = dot_nt(g0[...].astype(BF16), leaf[0, 0])
        v_in[0] = y0 * couple[0:1, 0:B]
        for k in range(1, n):
            v_copy(k).start()

    @pl.when(first)
    def _():
        g0[...] = f[0, :, 0:B]
        send_v()

    loads[2].wait()
    for b in range(1, per):
        at = (PLANES - 1) * plane + b * B
        out = dot_nt(f[0, :, at:at + B].astype(BF16), leaf[PLANES - 1, b])
        xint[0, :, at:at + B] = out
        t_out[:, b * B:(b + 1) * B] = out
    t_out[:, 0:B] = jnp.zeros((columns, B), F32)

    @pl.when(feeds)
    def _():
        t_copy.start()

    for k in range(1, n):
        map_copy(k).wait_recv()
    map0 = jnp.concatenate([maps[k, 0:1, :] for k in range(n)], axis=1)
    map15 = jnp.concatenate([maps[k, 1:2, :] for k in range(n)], axis=1)
    own0[...] = one_hot_rows(jnp.bitwise_and(map0, B - 1))
    hot15 = one_hot_rows(jnp.bitwise_and(map15, B - 1))
    own15[0:B, :] = hot15
    own15[B:2 * B, :] = hot15
    near = lax.broadcasted_iota(jnp.int32, (nh, n * B), 0) + me * nh
    is0 = near == jnp.right_shift(map0, 7)
    is15 = near == jnp.right_shift(map15, 7)

    def bulk():
        loads[3].wait()

        def one_plane(p, carry):
            for b in range(1, per):
                at = pl.multiple_of(p * plane + b * B, B)
                xint[0, :, pl.ds(at, B)] = dot_nt(f[0, :, pl.ds(at, B)].astype(BF16), leaf[p, b])
            return carry

        lax.fori_loop(1, PLANES - 1, one_plane, 0)

    @pl.when(later)
    def _():
        bulk()
        t_copy.wait_recv()
        for b in range(1, per):
            cut = slice(b * B, (b + 1) * B)
            g = f[0, :, cut] - coef[0:1, cut] * t_in[:, cut]
            xint[0, :, cut] = dot_nt(g.astype(BF16), leaf[0, b])
        l240_copy.wait_recv()
        aux_copy.wait_recv()
        l240 = l240_in[...].astype(BF16)
        for k in range(n):
            pick_copy(k).wait_recv()
        picked = pick_in[0]
        for k in range(1, n):
            picked = picked + pick_in[k]
        h = aux_in[0:columns, :] - aux_in[columns:columns + 1, :] * picked
        t = dot_nt(h.astype(BF16), l240)
        g0[...] = f[0, :, 0:B] - coef[0:1, 0:B] * t
        send_v()

    sres = jnp.concatenate(
        [fsep[0, r:r + 1, h * B:(h + 1) * B] for r in range(columns) for h in range(nh)], axis=0)
    sres = sres - base_out[me]
    for k in range(1, n):
        base_copy(k).wait_recv()
        sres = sres - base_in[k]
    for k in range(1, n):
        v_copy(k).wait_recv()
    v = jnp.concatenate([v_in[k] for k in range(n)], axis=1)
    v_high, v_low = split(v)
    rows = []
    for piece in (v_high.astype(F32), v_low.astype(F32)):
        for r in range(columns):
            rows.append(jnp.where(is0, piece[r:r + 1, :], 0.0))
    spread = dot_nt(jnp.concatenate(rows, axis=0).astype(BF16), own0[...])
    many = columns * nh
    sres = sres - (spread[0:many] + spread[many:2 * many])
    which = lax.rem(lax.broadcasted_iota(jnp.int32, (many, B), 0), nh)
    wide = jnp.concatenate([jnp.where(which == h, sres, 0.0) for h in range(nh)], axis=1).astype(BF16)
    x = dot_nt(wide, scat[...])
    xall[me] = x
    x_high, x_low = split(x)
    found = dot_nn(jnp.concatenate([x_high, x_low], axis=1), own15[...])
    for r in range(columns):
        line = jnp.sum(jnp.where(is15, found[r * nh:(r + 1) * nh], 0.0), axis=0, keepdims=True)
        for k in range(n):
            pick_out[k, r:r + 1, :] = line[:, k * B:(k + 1) * B]

    @pl.when(feeds)
    def _():
        for k in range(n):
            pick_copy(k).start()

    for k in range(1, n):
        x_copy(k).start()
    for r in range(columns):
        for h in range(nh):
            xsep[0, r:r + 1, h * B:(h + 1) * B] = x[r * nh + h:r * nh + h + 1, :]

    @pl.when(first)
    def _():
        bulk()
        for b in range(1, per):
            cut = slice(b * B, (b + 1) * B)
            xint[0, :, cut] = dot_nt(f[0, :, cut].astype(BF16), leaf[0, b])

    for k in range(1, n):
        x_copy(k).wait_recv()
    stacked = jnp.concatenate(
        [xall[:, r * nh:(r + 1) * nh, :].reshape(total, B) for r in range(columns)], axis=0)
    x_high, x_low = split(stacked)
    stacked = jnp.concatenate([x_high, x_low], axis=1)
    wide = 4 * B
    for c in range(PLANES * B // wide):
        cut = slice(c * wide, (c + 1) * wide)
        found = dot_nn(stacked, onehot[:, cut])
        mask = lax.broadcasted_iota(jnp.int32, (total, wide), 0) == high[:, cut]
        lines = [
            jnp.sum(jnp.where(mask, found[r * total:(r + 1) * total], 0.0), axis=0, keepdims=True)
            for r in range(columns)]
        fix = jnp.concatenate(lines, axis=0) * couple[0:1, cut]
        for q in range(wide // B):
            p = c * (wide // B) + q
            at = p * plane
            g = g0[...] if p == 0 else f[0, :, at:at + B]
            h = g - fix[:, q * B:(q + 1) * B]
            xint[0, :, at:at + B] = dot_nt(h.astype(BF16), leaf[p, 0])

    for k in range(1, n):
        map_copy(k).wait_send()
        base_copy(k).wait_send()
        v_copy(k).wait_send()
        x_copy(k).wait_send()

    @pl.when(feeds)
    def _():
        l240_copy.wait_send()
        aux_copy.wait_send()
        t_copy.wait_send()
        for k in range(n):
            pick_copy(k).wait_send()


def solution(mesh):
    S, n = mesh.shape["sweep"], mesh.shape["nd"]

    def shards(f_int, f_sep, leaf_inverse, sep_inverse, sep_map, couple, trace_coef):
        columns, leaf_rows = f_int.shape[1], f_int.shape[2]
        plane = leaf_rows // PLANES
        per = plane // B
        sep_rows = f_sep.shape[2]
        nh = sep_rows // B
        blocks = leaf_inverse.reshape(PLANES, per, B, B)
        vmem = pl.BlockSpec(memory_space=pltpu.VMEM)
        hbm = pl.BlockSpec(memory_space=pl.ANY)
        dma = pltpu.SemaphoreType.DMA
        x_int, x_sep = pl.pallas_call(
            functools.partial(kernel, S, n),
            out_shape=(jax.ShapeDtypeStruct(f_int.shape, F32), jax.ShapeDtypeStruct(f_sep.shape, F32)),
            in_specs=[hbm, hbm] + [vmem] * 5,
            out_specs=(vmem, vmem),
            scratch_shapes=[
                pltpu.VMEM((PLANES, per, B, B), BF16),
                pltpu.VMEM((1, columns, leaf_rows), F32),
                pltpu.VMEM((2 * B, PLANES * B), BF16),
                pltpu.VMEM((B, sep_rows), BF16),
                pltpu.VMEM((n, 2, B), jnp.int32),
                pltpu.VMEM((B, n * B), BF16),
                pltpu.VMEM((2 * B, n * B), BF16),
                pltpu.VMEM((n, columns * nh, B), F32),
                pltpu.VMEM((n, columns * nh, B), F32),
                pltpu.VMEM((n, columns, B), F32),
                pltpu.VMEM((n, columns, B), F32),
                pltpu.VMEM((n, columns, B), F32),
                pltpu.VMEM((n, columns * nh, B), F32),
                pltpu.VMEM((B, B), F32),
                pltpu.VMEM((B, B), F32),
                pltpu.VMEM((8, B), F32),
                pltpu.VMEM((8, B), F32),
                pltpu.VMEM((columns, plane), F32),
                pltpu.VMEM((columns, plane), F32),
                pltpu.VMEM((columns, B), F32),
                dma((4,)),
            ] + [dma((n,))] * 10 + [dma((3,))] * 2,
            compiler_params=pltpu.CompilerParams(
                collective_id=0, has_side_effects=True, vmem_limit_bytes=48 * 1024 * 1024),
        )(blocks, f_int, f_sep, sep_inverse, sep_map, couple, trace_coef)
        return x_int, x_sep

    placed = (
        P("sweep", None, "nd"),
        P("sweep", None, "nd"),
        P("sweep", "nd", None, None),
        P("sweep", "nd", None, None),
        P("sweep", "nd"),
        P("sweep", "nd"),
        P("sweep", "nd"),
    )
    return jax.shard_map(
        shards,
        mesh=mesh,
        in_specs=placed,
        out_specs=(P("sweep", None, "nd"), P("sweep", None, "nd")),
        check_vma=False,
    )
```

```python
import functools

import jax
import jax.numpy as jnp
from jax import lax
from jax.experimental import pallas as pl
from jax.experimental.pallas import tpu as pltpu
from jax.sharding import PartitionSpec as P

MESH = pl.DeviceIdType.MESH
PLANES = 16
B = 128
F32 = jnp.float32
BF16 = jnp.bfloat16


def dot_nt(a, b):
    return lax.dot_general(a, b, (((1,), (1,)), ((), ())), preferred_element_type=F32)


def dot_nn(a, b):
    return lax.dot_general(a, b, (((1,), (0,)), ((), ())), preferred_element_type=F32)


def split(x):
    high = x.astype(BF16)
    return high, (x - high.astype(F32)).astype(BF16)


def one_hot_rows(low, rows=B):
    shape = (rows, low.shape[1])
    return jnp.where(lax.broadcasted_iota(jnp.int32, shape, 0) == low, 1.0, 0.0).astype(BF16)


def kernel(S, n, leaf_hbm, f_hbm, fsep_hbm, sepinv_hbm, smap_hbm, couple_hbm, coef_hbm, xint, xsep,
           leaf, f, fsep, sepinv, smap, couple, coef, onehot, scat, own0, own15, base_out, base_in, v_in, pick_out, pick_in,
           xall, l240_out, l240_in, aux_out, aux_in, t_out, t_in, g0,
           load_sem, base_s, base_r, v_s, v_r, pick_s, pick_r, x_s, x_r, fwd_s, fwd_r):
    columns = f.shape[1]
    plane = f.shape[2] // PLANES
    per = plane // B
    nh = fsep.shape[2] // B
    total = n * nh
    s = lax.axis_index("sweep")
    me = lax.axis_index("nd")
    after = lax.rem(s + 1, S)
    before = lax.rem(s + S - 1, S)
    first = s == 0
    later = s > 0
    feeds = s < S - 1

    loads = [
        pltpu.make_async_copy(smap_hbm, smap, load_sem.at[4]),
        pltpu.make_async_copy(f_hbm, f, load_sem.at[0]),
        pltpu.make_async_copy(leaf_hbm.at[:, 0:1], leaf.at[:, 0:1], load_sem.at[1]),
        pltpu.make_async_copy(couple_hbm, couple, load_sem.at[5]),
        pltpu.make_async_copy(sepinv_hbm, sepinv, load_sem.at[6]),
        pltpu.make_async_copy(fsep_hbm, fsep, load_sem.at[7]),
        pltpu.make_async_copy(coef_hbm, coef, load_sem.at[8]),
        pltpu.make_async_copy(leaf_hbm.at[PLANES - 1:PLANES, 1:per], leaf.at[PLANES - 1:PLANES, 1:per], load_sem.at[2]),
        pltpu.make_async_copy(leaf_hbm.at[0:PLANES - 1, 1:per], leaf.at[0:PLANES - 1, 1:per], load_sem.at[3]),
    ]
    for load in loads:
        load.start()

    barrier = pltpu.get_barrier_semaphore()
    for k in range(1, n):
        pl.semaphore_signal(barrier, inc=1, device_id={"sweep": s, "nd": lax.rem(me + k, n)}, device_id_type=MESH)
    for k in range(n):
        other = lax.rem(me + k, n)
        pl.semaphore_signal(barrier, inc=1, device_id={"sweep": after, "nd": other}, device_id_type=MESH)
        pl.semaphore_signal(barrier, inc=1, device_id={"sweep": before, "nd": other}, device_id_type=MESH)

    def to(src, dst, send, recv, sweep, nd):
        return pltpu.make_async_remote_copy(
            src_ref=src, dst_ref=dst, send_sem=send, recv_sem=recv,
            device_id={"sweep": sweep, "nd": nd}, device_id_type=MESH)

    def base_copy(k):
        other = lax.rem(me + k, n)
        return to(base_out.at[other], base_in.at[k], base_s.at[k], base_r.at[k], s, other)

    def v_copy(k):
        return to(v_in.at[0], v_in.at[k], v_s.at[k], v_r.at[k], s, lax.rem(me + k, n))

    def pick_copy(k):
        return to(pick_out.at[k], pick_in.at[k], pick_s.at[k], pick_r.at[k], after, lax.rem(me + n - k, n))

    def x_copy(k):
        return to(xall.at[me], xall.at[me], x_s.at[k], x_r.at[k], s, lax.rem(me + k, n))

    l240_copy = to(l240_out, l240_in, fwd_s.at[0], fwd_r.at[0], after, me)
    aux_copy = to(aux_out, aux_in, fwd_s.at[1], fwd_r.at[1], after, me)
    t_copy = to(t_out, t_in, fwd_s.at[2], fwd_r.at[2], after, me)

    loads[0].wait()
    row_map = smap[0:1, :]
    low = jnp.bitwise_and(row_map, B - 1)
    high = jnp.right_shift(row_map, 7)
    hot = one_hot_rows(low)
    onehot[0:B, :] = hot
    onehot[B:2 * B, :] = hot

    for load in loads[1:4]:
        load.wait()
    aux_out[0:columns, :] = f[0, :, (PLANES - 1) * plane:(PLANES - 1) * plane + B]
    aux_out[columns:columns + 1, :] = couple[0:1, (PLANES - 1) * B:PLANES * B]
    l240_out[...] = leaf[PLANES - 1, 0].astype(F32)

    parts = []
    for p in range(PLANES):
        g = f[0, :, p * plane:p * plane + B].astype(BF16)
        parts.append(dot_nt(g, leaf[p, 0]) * couple[0:1, p * B:(p + 1) * B])
    parts[0] = jnp.where(first, parts[0], 0.0)
    vals = jnp.concatenate(parts, axis=1)
    v_high, v_low = split(vals)
    v_high, v_low = v_high.astype(F32), v_low.astype(F32)
    is_high = lax.broadcasted_iota(jnp.int32, (total, PLANES * B), 0) == high
    rows = []
    for piece in (v_high, v_low):
        for r in range(columns):
            rows.append(jnp.where(is_high, piece[r:r + 1, :], 0.0).astype(BF16))
    spread = dot_nt(jnp.concatenate(rows, axis=0), onehot[0:B, :])
    for r in range(columns):
        both = spread[r * total:(r + 1) * total] + spread[(columns + r) * total:(columns + r + 1) * total]
        base_out[:, r * nh:(r + 1) * nh, :] = both.reshape(n, nh, B)
    many = columns * nh
    ends = jnp.concatenate(
        [smap[0:1, 0:B], smap[0:1, (PLANES - 1) * B:PLANES * B], jnp.zeros((6, B), jnp.int32)], axis=0).astype(F32)
    for o in range(n):
        base_out[o, many:many + 8, :] = ends
    pl.semaphore_wait(barrier, 3 * n - 1)
    for k in range(1, n):
        base_copy(k).start()

    @pl.when(feeds)
    def _():
        l240_copy.start()
        aux_copy.start()

    def send_v():
        y0 = dot_nt(g0[...].astype(BF16), leaf[0, 0])
        v_in[0] = y0 * couple[0:1, 0:B]
        for k in range(1, n):
            v_copy(k).start()

    @pl.when(first)
    def _():
        g0[...] = f[0, :, 0:B]
        v_in[...] = jnp.zeros_like(v_in)

    for load in loads[4:7]:
        load.wait()
    for h in range(nh):
        scat[:, h * B:(h + 1) * B] = sepinv[0, h]

    loads[7].wait()
    for b in range(1, per):
        at = (PLANES - 1) * plane + b * B
        out = dot_nt(f[0, :, at:at + B].astype(BF16), leaf[PLANES - 1, b])
        xint[0, :, at:at + B] = out
        t_out[:, b * B:(b + 1) * B] = out
    t_out[:, 0:B] = jnp.zeros((columns, B), F32)

    @pl.when(feeds)
    def _():
        t_copy.start()

    sres = jnp.concatenate(
        [fsep[0, r:r + 1, h * B:(h + 1) * B] for r in range(columns) for h in range(nh)], axis=0)
    own = base_out[me]
    sres = sres - own[0:many]
    for k in range(1, n):
        base_copy(k).wait_recv()
        sres = sres - base_in[k, 0:many, :]
    map0 = jnp.concatenate(
        [own[many:many + 1]] + [base_in[k, many:many + 1, :] for k in range(1, n)], axis=1).astype(jnp.int32)
    map15 = jnp.concatenate(
        [own[many + 1:many + 2]] + [base_in[k, many + 1:many + 2, :] for k in range(1, n)], axis=1).astype(jnp.int32)
    own0[...] = one_hot_rows(jnp.bitwise_and(map0, B - 1))
    hot15 = one_hot_rows(jnp.bitwise_and(map15, B - 1))
    own15[0:B, :] = hot15
    own15[B:2 * B, :] = hot15
    near = lax.broadcasted_iota(jnp.int32, (nh, n * B), 0) + me * nh
    is0 = near == jnp.right_shift(map0, 7)
    is15 = near == jnp.right_shift(map15, 7)

    def bulk():
        loads[8].wait()

        def one_plane(p, carry):
            for b in range(1, per):
                at = pl.multiple_of(p * plane + b * B, B)
                xint[0, :, pl.ds(at, B)] = dot_nt(f[0, :, pl.ds(at, B)].astype(BF16), leaf[p, b])
            return carry

        lax.fori_loop(1, PLANES - 1, one_plane, 0)

    @pl.when(later)
    def _():
        bulk()
        t_copy.wait_recv()
        for b in range(1, per):
            cut = slice(b * B, (b + 1) * B)
            g = f[0, :, cut] - coef[0:1, cut] * t_in[:, cut]
            xint[0, :, cut] = dot_nt(g.astype(BF16), leaf[0, b])
        l240_copy.wait_recv()
        aux_copy.wait_recv()
        l240 = l240_in[...].astype(BF16)
        for k in range(n):
            pick_copy(k).wait_recv()
        picked = pick_in[0]
        for k in range(1, n):
            picked = picked + pick_in[k]
        h = aux_in[0:columns, :] - aux_in[columns:columns + 1, :] * picked
        t = dot_nt(h.astype(BF16), l240)
        g0[...] = f[0, :, 0:B] - coef[0:1, 0:B] * t
        send_v()

    @pl.when(later)
    def _():
        for k in range(1, n):
            v_copy(k).wait_recv()

    v = jnp.concatenate([v_in[k] for k in range(n)], axis=1)
    v_high, v_low = split(v)
    rows = []
    for piece in (v_high.astype(F32), v_low.astype(F32)):
        for r in range(columns):
            rows.append(jnp.where(is0, piece[r:r + 1, :], 0.0))
    spread = dot_nt(jnp.concatenate(rows, axis=0).astype(BF16), own0[...])
    sres = sres - (spread[0:many] + spread[many:2 * many])
    which = lax.rem(lax.broadcasted_iota(jnp.int32, (many, B), 0), nh)
    wide = jnp.concatenate([jnp.where(which == h, sres, 0.0) for h in range(nh)], axis=1).astype(BF16)
    x = dot_nt(wide, scat[...])
    xall[me] = x
    x_high, x_low = split(x)
    found = dot_nn(jnp.concatenate([x_high, x_low], axis=1), own15[...])
    for r in range(columns):
        line = jnp.sum(jnp.where(is15, found[r * nh:(r + 1) * nh], 0.0), axis=0, keepdims=True)
        for k in range(n):
            pick_out[k, r:r + 1, :] = line[:, k * B:(k + 1) * B]

    @pl.when(feeds)
    def _():
        for k in range(n):
            pick_copy(k).start()

    for k in range(1, n):
        x_copy(k).start()
    for r in range(columns):
        for h in range(nh):
            xsep[0, r:r + 1, h * B:(h + 1) * B] = x[r * nh + h:r * nh + h + 1, :]

    @pl.when(first)
    def _():
        bulk()
        for b in range(1, per):
            cut = slice(b * B, (b + 1) * B)
            xint[0, :, cut] = dot_nt(f[0, :, cut].astype(BF16), leaf[0, b])

    for k in range(1, n):
        x_copy(k).wait_recv()
    stacked = jnp.concatenate(
        [xall[:, r * nh:(r + 1) * nh, :].reshape(total, B) for r in range(columns)], axis=0)
    x_high, x_low = split(stacked)
    stacked = jnp.concatenate([x_high, x_low], axis=1)
    wide = 4 * B
    for c in range(PLANES * B // wide):
        cut = slice(c * wide, (c + 1) * wide)
        found = dot_nn(stacked, onehot[:, cut])
        mask = lax.broadcasted_iota(jnp.int32, (total, wide), 0) == high[:, cut]
        lines = [
            jnp.sum(jnp.where(mask, found[r * total:(r + 1) * total], 0.0), axis=0, keepdims=True)
            for r in range(columns)]
        fix = jnp.concatenate(lines, axis=0) * couple[0:1, cut]
        for q in range(wide // B):
            p = c * (wide // B) + q
            at = p * plane
            g = g0[...] if p == 0 else f[0, :, at:at + B]
            h = g - fix[:, q * B:(q + 1) * B]
            xint[0, :, at:at + B] = dot_nt(h.astype(BF16), leaf[p, 0])

    for k in range(1, n):
        base_copy(k).wait_send()
        x_copy(k).wait_send()

    @pl.when(later)
    def _():
        for k in range(1, n):
            v_copy(k).wait_send()

    @pl.when(feeds)
    def _():
        l240_copy.wait_send()
        aux_copy.wait_send()
        t_copy.wait_send()
        for k in range(n):
            pick_copy(k).wait_send()


def solution(mesh):
    S, n = mesh.shape["sweep"], mesh.shape["nd"]

    def shards(f_int, f_sep, leaf_inverse, sep_inverse, sep_map, couple, trace_coef):
        columns, leaf_rows = f_int.shape[1], f_int.shape[2]
        plane = leaf_rows // PLANES
        per = plane // B
        sep_rows = f_sep.shape[2]
        nh = sep_rows // B
        blocks = leaf_inverse.reshape(PLANES, per, B, B)
        vmem = pl.BlockSpec(memory_space=pltpu.VMEM)
        hbm = pl.BlockSpec(memory_space=pltpu.HBM)
        dma = pltpu.SemaphoreType.DMA
        x_int, x_sep = pl.pallas_call(
            functools.partial(kernel, S, n),
            out_shape=(pltpu.VMEM(f_int.shape, F32), pltpu.VMEM(f_sep.shape, F32)),
            in_specs=[hbm] * 7,
            out_specs=(vmem, vmem),
            scratch_shapes=[
                pltpu.VMEM((PLANES, per, B, B), BF16),
                pltpu.VMEM((1, columns, leaf_rows), F32),
                pltpu.VMEM(f_sep.shape, F32),
                pltpu.VMEM(sep_inverse.shape, BF16),
                pltpu.VMEM(sep_map.shape, jnp.int32),
                pltpu.VMEM(couple.shape, F32),
                pltpu.VMEM(trace_coef.shape, F32),
                pltpu.VMEM((2 * B, PLANES * B), BF16),
                pltpu.VMEM((B, sep_rows), BF16),
                pltpu.VMEM((B, n * B), BF16),
                pltpu.VMEM((2 * B, n * B), BF16),
                pltpu.VMEM((n, columns * nh + 8, B), F32),
                pltpu.VMEM((n, columns * nh + 8, B), F32),
                pltpu.VMEM((n, columns, B), F32),
                pltpu.VMEM((n, columns, B), F32),
                pltpu.VMEM((n, columns, B), F32),
                pltpu.VMEM((n, columns * nh, B), F32),
                pltpu.VMEM((B, B), F32),
                pltpu.VMEM((B, B), F32),
                pltpu.VMEM((8, B), F32),
                pltpu.VMEM((8, B), F32),
                pltpu.VMEM((columns, plane), F32),
                pltpu.VMEM((columns, plane), F32),
                pltpu.VMEM((columns, B), F32),
                dma((9,)),
            ] + [dma((n,))] * 8 + [dma((3,))] * 2,
            compiler_params=pltpu.CompilerParams(
                collective_id=0, has_side_effects=True, vmem_limit_bytes=56 * 1024 * 1024),
        )(blocks, f_int, f_sep, sep_inverse, sep_map, couple, trace_coef)
        return x_int, x_sep

    placed = (
        P("sweep", None, "nd"),
        P("sweep", None, "nd"),
        P("sweep", "nd", None, None),
        P("sweep", "nd", None, None),
        P("sweep", "nd"),
        P("sweep", "nd"),
        P("sweep", "nd"),
    )
    return jax.shard_map(
        shards,
        mesh=mesh,
        in_specs=placed,
        out_specs=(P("sweep", None, "nd"), P("sweep", None, "nd")),
        check_vma=False,
    )
```

```python
import functools

import jax
import jax.numpy as jnp
from jax import lax
from jax.experimental import pallas as pl
from jax.experimental.pallas import tpu as pltpu
from jax.sharding import PartitionSpec as P

MESH = pl.DeviceIdType.MESH
PLANES = 16
B = 128
F32 = jnp.float32
BF16 = jnp.bfloat16


def dot_nt(a, b):
    return lax.dot_general(a, b, (((1,), (1,)), ((), ())), preferred_element_type=F32)


def dot_nn(a, b):
    return lax.dot_general(a, b, (((1,), (0,)), ((), ())), preferred_element_type=F32)


def split(x):
    high = x.astype(BF16)
    return high, (x - high.astype(F32)).astype(BF16)


def one_hot_rows(low, rows=B):
    shape = (rows, low.shape[1])
    return jnp.where(lax.broadcasted_iota(jnp.int32, shape, 0) == low, 1.0, 0.0).astype(BF16)


def kernel(S, n, leaf_hbm, f_hbm, fsep_hbm, sepinv_hbm, smap_hbm, couple_hbm, coef_hbm, xint, xsep,
           leaf, f, fsep, sepinv, smap, couple, coef, onehot, scat, own0, own15, base_out, base_in, v_in, pick_out, pick_in,
           xall, l240_out, l240_in, aux_out, aux_in, t_out, t_in, g0,
           load_sem, base_s, base_r, v_s, v_r, pick_s, pick_r, x_s, x_r, fwd_s, fwd_r):
    columns = f.shape[1]
    plane = f.shape[2] // PLANES
    per = plane // B
    nh = fsep.shape[2] // B
    total = n * nh
    s = lax.axis_index("sweep")
    me = lax.axis_index("nd")
    after = lax.rem(s + 1, S)
    before = lax.rem(s + S - 1, S)
    first = s == 0
    later = s > 0
    feeds = s < S - 1

    loads = [
        pltpu.make_async_copy(smap_hbm, smap, load_sem.at[4]),
        pltpu.make_async_copy(f_hbm, f, load_sem.at[0]),
        pltpu.make_async_copy(leaf_hbm.at[:, 0:1], leaf.at[:, 0:1], load_sem.at[1]),
        pltpu.make_async_copy(couple_hbm, couple, load_sem.at[5]),
        pltpu.make_async_copy(sepinv_hbm, sepinv, load_sem.at[6]),
        pltpu.make_async_copy(fsep_hbm, fsep, load_sem.at[7]),
        pltpu.make_async_copy(coef_hbm, coef, load_sem.at[8]),
        pltpu.make_async_copy(leaf_hbm.at[PLANES - 1:PLANES, 1:per], leaf.at[PLANES - 1:PLANES, 1:per], load_sem.at[2]),
        pltpu.make_async_copy(leaf_hbm.at[0:PLANES - 1, 1:per], leaf.at[0:PLANES - 1, 1:per], load_sem.at[3]),
    ]
    for load in loads:
        load.start()

    barrier = pltpu.get_barrier_semaphore()
    for k in range(1, n):
        pl.semaphore_signal(barrier, inc=1, device_id={"sweep": s, "nd": lax.rem(me + k, n)}, device_id_type=MESH)
    for k in range(n):
        other = lax.rem(me + k, n)
        pl.semaphore_signal(barrier, inc=1, device_id={"sweep": after, "nd": other}, device_id_type=MESH)
        pl.semaphore_signal(barrier, inc=1, device_id={"sweep": before, "nd": other}, device_id_type=MESH)

    def to(src, dst, send, recv, sweep, nd):
        return pltpu.make_async_remote_copy(
            src_ref=src, dst_ref=dst, send_sem=send, recv_sem=recv,
            device_id={"sweep": sweep, "nd": nd}, device_id_type=MESH)

    def base_copy(k):
        other = lax.rem(me + k, n)
        return to(base_out.at[other], base_in.at[k], base_s.at[k], base_r.at[k], s, other)

    def v_copy(k):
        return to(v_in.at[0], v_in.at[k], v_s.at[k], v_r.at[k], s, lax.rem(me + k, n))

    def pick_copy(k):
        return to(pick_out.at[k], pick_in.at[k], pick_s.at[k], pick_r.at[k], after, lax.rem(me + n - k, n))

    def x_copy(k):
        return to(xall.at[me], xall.at[me], x_s.at[k], x_r.at[k], s, lax.rem(me + k, n))

    l240_copy = to(l240_out, l240_in, fwd_s.at[0], fwd_r.at[0], after, me)
    aux_copy = to(aux_out, aux_in, fwd_s.at[1], fwd_r.at[1], after, me)
    t_copy = to(t_out, t_in, fwd_s.at[2], fwd_r.at[2], after, me)

    loads[0].wait()
    row_map = smap[0:1, :]
    low = jnp.bitwise_and(row_map, B - 1)
    high = jnp.right_shift(row_map, 7)
    hot = one_hot_rows(low)
    onehot[0:B, :] = hot
    onehot[B:2 * B, :] = hot

    for load in loads[1:4]:
        load.wait()
    aux_out[0:columns, :] = f[0, :, (PLANES - 1) * plane:(PLANES - 1) * plane + B]
    aux_out[columns:columns + 1, :] = couple[0:1, (PLANES - 1) * B:PLANES * B]
    l240_out[...] = leaf[PLANES - 1, 0].astype(F32)

    parts = []
    for p in range(PLANES):
        g = f[0, :, p * plane:p * plane + B].astype(BF16)
        parts.append(dot_nt(g, leaf[p, 0]) * couple[0:1, p * B:(p + 1) * B])
    parts[0] = jnp.where(first, parts[0], 0.0)
    vals = jnp.concatenate(parts, axis=1)
    v_high, v_low = split(vals)
    v_high, v_low = v_high.astype(F32), v_low.astype(F32)
    is_high = lax.broadcasted_iota(jnp.int32, (total, PLANES * B), 0) == high
    rows = []
    for piece in (v_high, v_low):
        for r in range(columns):
            rows.append(jnp.where(is_high, piece[r:r + 1, :], 0.0).astype(BF16))
    spread = dot_nt(jnp.concatenate(rows, axis=0), onehot[0:B, :])
    for r in range(columns):
        both = spread[r * total:(r + 1) * total] + spread[(columns + r) * total:(columns + r + 1) * total]
        base_out[:, r * nh:(r + 1) * nh, :] = both.reshape(n, nh, B)
    many = columns * nh
    ends = jnp.concatenate(
        [smap[0:1, 0:B], smap[0:1, (PLANES - 1) * B:PLANES * B], jnp.zeros((6, B), jnp.int32)], axis=0).astype(F32)
    for o in range(n):
        base_out[o, many:many + 8, :] = ends
    pl.semaphore_wait(barrier, 3 * n - 1)
    for k in range(1, n):
        base_copy(k).start()

    @pl.when(feeds)
    def _():
        l240_copy.start()
        aux_copy.start()

    def send_v():
        y0 = dot_nt(g0[...].astype(BF16), leaf[0, 0])
        v_in[0] = y0 * couple[0:1, 0:B]
        for k in range(1, n):
            v_copy(k).start()

    @pl.when(first)
    def _():
        g0[...] = f[0, :, 0:B]
        v_in[...] = jnp.zeros_like(v_in)

    for load in loads[4:7]:
        load.wait()
    for h in range(nh):
        scat[:, h * B:(h + 1) * B] = sepinv[0, h]

    loads[7].wait()
    for b in range(1, per):
        at = (PLANES - 1) * plane + b * B
        out = dot_nt(f[0, :, at:at + B].astype(BF16), leaf[PLANES - 1, b])
        xint[0, :, at:at + B] = out
        t_out[:, b * B:(b + 1) * B] = out
    t_out[:, 0:B] = jnp.zeros((columns, B), F32)

    @pl.when(feeds)
    def _():
        t_copy.start()

    sres = jnp.concatenate(
        [fsep[0, r:r + 1, h * B:(h + 1) * B] for r in range(columns) for h in range(nh)], axis=0)
    own = base_out[me]
    sres = sres - own[0:many]
    for k in range(1, n):
        base_copy(k).wait_recv()
        sres = sres - base_in[k, 0:many, :]
    map0 = jnp.concatenate(
        [own[many:many + 1]] + [base_in[k, many:many + 1, :] for k in range(1, n)], axis=1).astype(jnp.int32)
    map15 = jnp.concatenate(
        [own[many + 1:many + 2]] + [base_in[k, many + 1:many + 2, :] for k in range(1, n)], axis=1).astype(jnp.int32)
    own0[...] = one_hot_rows(jnp.bitwise_and(map0, B - 1))
    hot15 = one_hot_rows(jnp.bitwise_and(map15, B - 1))
    own15[0:B, :] = hot15
    own15[B:2 * B, :] = hot15
    near = lax.broadcasted_iota(jnp.int32, (nh, n * B), 0) + me * nh
    is0 = near == jnp.right_shift(map0, 7)
    is15 = near == jnp.right_shift(map15, 7)

    def bulk():
        loads[8].wait()

        def one_plane(p, carry):
            for b in range(1, per):
                at = pl.multiple_of(p * plane + b * B, B)
                xint[0, :, pl.ds(at, B)] = dot_nt(f[0, :, pl.ds(at, B)].astype(BF16), leaf[p, b])
            return carry

        lax.fori_loop(1, PLANES - 1, one_plane, 0)

    @pl.when(later)
    def _():
        bulk()
        t_copy.wait_recv()
        for b in range(1, per):
            cut = slice(b * B, (b + 1) * B)
            g = f[0, :, cut] - coef[0:1, cut] * t_in[:, cut]
            xint[0, :, cut] = dot_nt(g.astype(BF16), leaf[0, b])
        l240_copy.wait_recv()
        aux_copy.wait_recv()
        l240 = l240_in[...].astype(BF16)
        for k in range(n):
            pick_copy(k).wait_recv()
        picked = pick_in[0]
        for k in range(1, n):
            picked = picked + pick_in[k]
        h = aux_in[0:columns, :] - aux_in[columns:columns + 1, :] * picked
        t = dot_nt(h.astype(BF16), l240)
        g0[...] = f[0, :, 0:B] - coef[0:1, 0:B] * t
        send_v()

    @pl.when(later)
    def _():
        for k in range(1, n):
            v_copy(k).wait_recv()

    v = jnp.concatenate([v_in[k] for k in range(n)], axis=1)
    v_high, v_low = split(v)
    rows = []
    for piece in (v_high.astype(F32), v_low.astype(F32)):
        for r in range(columns):
            rows.append(jnp.where(is0, piece[r:r + 1, :], 0.0))
    spread = dot_nt(jnp.concatenate(rows, axis=0).astype(BF16), own0[...])
    sres = sres - (spread[0:many] + spread[many:2 * many])
    which = lax.rem(lax.broadcasted_iota(jnp.int32, (many, B), 0), nh)
    wide = jnp.concatenate([jnp.where(which == h, sres, 0.0) for h in range(nh)], axis=1).astype(BF16)
    x = dot_nt(wide, scat[...])
    xall[me] = x

    def send_x():
        for k in range(1, n):
            x_copy(k).start()

    @pl.when(jnp.logical_not(feeds))
    def _():
        send_x()

    @pl.when(feeds)
    def _():
        x_high, x_low = split(x)
        found = dot_nn(jnp.concatenate([x_high, x_low], axis=1), own15[...])
        for r in range(columns):
            line = jnp.sum(jnp.where(is15, found[r * nh:(r + 1) * nh], 0.0), axis=0, keepdims=True)
            for k in range(n):
                pick_out[k, r:r + 1, :] = line[:, k * B:(k + 1) * B]
        for k in range(n):
            pick_copy(k).start()
        send_x()

    for r in range(columns):
        for h in range(nh):
            xsep[0, r:r + 1, h * B:(h + 1) * B] = x[r * nh + h:r * nh + h + 1, :]

    @pl.when(first)
    def _():
        bulk()
        for b in range(1, per):
            cut = slice(b * B, (b + 1) * B)
            xint[0, :, cut] = dot_nt(f[0, :, cut].astype(BF16), leaf[0, b])

    for k in range(1, n):
        x_copy(k).wait_recv()
    stacked = jnp.concatenate(
        [xall[:, r * nh:(r + 1) * nh, :].reshape(total, B) for r in range(columns)], axis=0)
    x_high, x_low = split(stacked)
    stacked = jnp.concatenate([x_high, x_low], axis=1)
    wide = 4 * B
    for c in range(PLANES * B // wide):
        cut = slice(c * wide, (c + 1) * wide)
        found = dot_nn(stacked, onehot[:, cut])
        mask = lax.broadcasted_iota(jnp.int32, (total, wide), 0) == high[:, cut]
        lines = [
            jnp.sum(jnp.where(mask, found[r * total:(r + 1) * total], 0.0), axis=0, keepdims=True)
            for r in range(columns)]
        fix = jnp.concatenate(lines, axis=0) * couple[0:1, cut]
        for q in range(wide // B):
            p = c * (wide // B) + q
            at = p * plane
            g = g0[...] if p == 0 else f[0, :, at:at + B]
            h = g - fix[:, q * B:(q + 1) * B]
            xint[0, :, at:at + B] = dot_nt(h.astype(BF16), leaf[p, 0])

    for k in range(1, n):
        base_copy(k).wait_send()
        x_copy(k).wait_send()

    @pl.when(later)
    def _():
        for k in range(1, n):
            v_copy(k).wait_send()

    @pl.when(feeds)
    def _():
        l240_copy.wait_send()
        aux_copy.wait_send()
        t_copy.wait_send()
        for k in range(n):
            pick_copy(k).wait_send()


def solution(mesh):
    S, n = mesh.shape["sweep"], mesh.shape["nd"]

    def shards(f_int, f_sep, leaf_inverse, sep_inverse, sep_map, couple, trace_coef):
        columns, leaf_rows = f_int.shape[1], f_int.shape[2]
        plane = leaf_rows // PLANES
        per = plane // B
        sep_rows = f_sep.shape[2]
        nh = sep_rows // B
        blocks = leaf_inverse.reshape(PLANES, per, B, B)
        vmem = pl.BlockSpec(memory_space=pltpu.VMEM)
        hbm = pl.BlockSpec(memory_space=pltpu.HBM)
        dma = pltpu.SemaphoreType.DMA
        x_int, x_sep = pl.pallas_call(
            functools.partial(kernel, S, n),
            out_shape=(pltpu.VMEM(f_int.shape, F32), pltpu.VMEM(f_sep.shape, F32)),
            in_specs=[hbm] * 7,
            out_specs=(vmem, vmem),
            scratch_shapes=[
                pltpu.VMEM((PLANES, per, B, B), BF16),
                pltpu.VMEM((1, columns, leaf_rows), F32),
                pltpu.VMEM(f_sep.shape, F32),
                pltpu.VMEM(sep_inverse.shape, BF16),
                pltpu.VMEM(sep_map.shape, jnp.int32),
                pltpu.VMEM(couple.shape, F32),
                pltpu.VMEM(trace_coef.shape, F32),
                pltpu.VMEM((2 * B, PLANES * B), BF16),
                pltpu.VMEM((B, sep_rows), BF16),
                pltpu.VMEM((B, n * B), BF16),
                pltpu.VMEM((2 * B, n * B), BF16),
                pltpu.VMEM((n, columns * nh + 8, B), F32),
                pltpu.VMEM((n, columns * nh + 8, B), F32),
                pltpu.VMEM((n, columns, B), F32),
                pltpu.VMEM((n, columns, B), F32),
                pltpu.VMEM((n, columns, B), F32),
                pltpu.VMEM((n, columns * nh, B), F32),
                pltpu.VMEM((B, B), F32),
                pltpu.VMEM((B, B), F32),
                pltpu.VMEM((8, B), F32),
                pltpu.VMEM((8, B), F32),
                pltpu.VMEM((columns, plane), F32),
                pltpu.VMEM((columns, plane), F32),
                pltpu.VMEM((columns, B), F32),
                dma((9,)),
            ] + [dma((n,))] * 8 + [dma((3,))] * 2,
            compiler_params=pltpu.CompilerParams(
                collective_id=0, has_side_effects=True, vmem_limit_bytes=56 * 1024 * 1024),
        )(blocks, f_int, f_sep, sep_inverse, sep_map, couple, trace_coef)
        return x_int, x_sep

    placed = (
        P("sweep", None, "nd"),
        P("sweep", None, "nd"),
        P("sweep", "nd", None, None),
        P("sweep", "nd", None, None),
        P("sweep", "nd"),
        P("sweep", "nd"),
        P("sweep", "nd"),
    )
    return jax.shard_map(
        shards,
        mesh=mesh,
        in_specs=placed,
        out_specs=(P("sweep", None, "nd"), P("sweep", None, "nd")),
        check_vma=False,
    )
```
